32 devices in a mesh: dp: 8 (over y, x, core), tensor: 4 (over z).
Axes of the slice: x: 2, y: 2, z: 4, core: 2. Of those that a mesh axis runs over, the one named last changes fastest.
Arguments:
- tokens_in: bfloat16 [8192, 768], P('dp'), may hold values from -6 to 6
- segments: int32 [8, 1024], P('dp'), may hold values from 0 to 3, never falling along the last dimension, each value on 1 to 512 neighbouring positions
- ln1_gain: float32 [768], replicated, may hold values from 0.1 to 1.9
- ln1_shift: float32 [768], replicated, may hold values from -3 to 3
- w_query: bfloat16 [768, 768], P(None, 'tensor'), may hold values from -0.21875 to 0.21875
- bias_query: float32 [768], P('tensor'), may hold values from -3 to 3
- w_key: bfloat16 [768, 768], P(None, 'tensor'), may hold values from -0.21875 to 0.21875
- w_value: bfloat16 [768, 768], P(None, 'tensor'), may hold values from -0.21875 to 0.21875
- bias_value: float32 [768], P('tensor'), may hold values from -3 to 3
- w_out: bfloat16 [768, 768], P('tensor'), may hold values from -1.75 to 1.75
- bias_out: float32 [768], replicated, may hold values from -3 to 3
- ln2_gain: float32 [768], replicated, may hold values from 0.1 to 1.9
- ln2_shift: float32 [768], replicated, may hold values from -3 to 3
- w_up: bfloat16 [768, 3072], P(None, 'tensor'), may hold values from -0.21875 to 0.21875
- bias_up: float32 [3072], P('tensor'), may hold values from -3 to 3
- w_down: bfloat16 [3072, 768], P('tensor'), may hold values from -0.109375 to 0.109375
- bias_down: float32 [768], replicated, may hold values from -3 to 3
- cotangent: bfloat16 [8192, 768], P('dp'), may hold values from -6 to 6
Outputs:
- output: bfloat16 [8192, 768], P('dp')
- grad_input: float32 [8192, 768], P('dp')
- grad_ln1_gain: float32 [768], replicated
- grad_ln1_shift: float32 [768], replicated
- grad_w_query: float32 [768, 768], P(None, 'tensor')
- grad_bias_query: float32 [768], P('tensor')
- grad_w_key: float32 [768, 768], P(None, 'tensor')
- grad_w_value: float32 [768, 768], P(None, 'tensor')
- grad_bias_value: float32 [768], P('tensor')
- grad_w_out: float32 [768, 768], P('tensor')
- grad_bias_out: float32 [768], replicated
- grad_ln2_gain: float32 [768], replicated
- grad_ln2_shift: float32 [768], replicated
- grad_w_up: float32 [768, 3072], P(None, 'tensor')
- grad_bias_up: float32 [3072], P('tensor')
- grad_w_down: float32 [3072, 768], P('tensor')
- grad_bias_down: float32 [768], replicated
The draws below stay inside these ranges and needn't reach their ends.
Inputs may be any that keep to these rules, and one draw needn't show every extreme that they name: `segments`: within each sequence the document numbers never fall, each document holds 1 to half of 1024 tokens, and one holds exactly half of 1024.
All inputs are finite; a program needn't handle non-finite values.
Results may differ from the reference program's by a relative error of at most 0.012.
The reference program's roundings to bfloat16 on the way count: a program that leaves them out, or rounds other values in their place, can miss the bound.
Values sent between devices are 32-bit elements; how exact they have to be, the bound alone decides.
A program may use at most 128 MiB of HBM per device.

```python
import math
import jax
import jax.numpy as jnp
import numpy as np
from jax import lax

D = 768
H = 12
HD = 64
FF = 3072
SEQ = 1024
SEQS = 8
TOKENS = 8192
DOCS = 4


def block_scale(stream_key, dims, cuts, low, top_value):
    loudness, own = 1.0, jax.random.fold_in(stream_key, 6)
    for axis_at, parts in cuts:
        heights = jnp.exp(jax.random.uniform(jax.random.fold_in(own, axis_at), (parts,), jnp.float32, low / len(cuts), top_value / len(cuts)))
        loudness = loudness * jnp.repeat(heights, dims[axis_at] // parts).reshape([-1 if axis == axis_at else 1 for axis in range(len(dims))])
    return loudness


def split_up(number_of, total, limit, lean):
    loads = [(1 << 20) // math.isqrt(grade ** lean) + 1 for grade in range(2, number_of + 1)]
    spare, given = total - limit - (number_of - 1), [1] * (number_of - 1)
    while spare > 0:
        free = [i for i in range(number_of - 1) if given[i] < limit]
        mass, left = sum([loads[i] for i in free]), spare
        for i in free:
            addition = min(limit - given[i], max(1, left * loads[i] // mass), spare)
            given[i] = given[i] + addition
            spare = spare - addition
    return np.array([limit] + given)


def uneven_parts(stream_key, amount, total, most, skew):
    if amount == 2:
        one = jax.random.randint(stream_key, (), max(1, total - most), min(most, total - 1) + 1)
        return jnp.stack([one, total - one])
    sizes = jnp.asarray(split_up(amount, total, most, skew), jnp.int32)
    couples = (amount - 1) // 2
    donor, taker = sizes[1:1 + 2 * couples:2], sizes[2:2 + 2 * couples:2]
    slack = jnp.minimum(donor - 1, most - taker)
    shifted = jax.random.randint(jax.random.fold_in(stream_key, 1), (couples,), 0, 1 << 20) % (slack + 1)
    sizes = sizes.at[1:1 + 2 * couples:2].set(donor - shifted).at[2:2 + 2 * couples:2].set(taker + shifted)
    return sizes[jax.random.permutation(jax.random.fold_in(stream_key, 2), amount)]


def gaussian(rng, dims, scale, limit, split=(), held_as=jnp.bfloat16):
    values = jax.random.normal(rng, dims, jnp.float32) * scale
    if len(split) > 0:
        values = block_scale(rng, dims, split, -0.22, 0.18) * values
    return jnp.clip(values, min=-limit, max=limit).astype(held_as)


def setup_inputs(seed: int = 0) -> dict:
    arg_keys = jax.random.split(jax.random.key(seed), 19)
    return {
        "tokens_in": gaussian(arg_keys[0], (TOKENS, D), 1.0, 6.0, ((0, 8),)),
        "segments": jax.vmap(lambda own: jnp.searchsorted(jnp.cumsum(uneven_parts(own, DOCS, SEQ, SEQ // 2, 0)), jnp.arange(SEQ), side="right"))(jax.random.split(arg_keys[1], SEQS)).reshape((SEQS, SEQ)).astype(jnp.int32),
        "ln1_gain": jnp.clip(1.0 + 0.18 * jax.random.normal(arg_keys[2], (D,), jnp.float32), 0.1, 1.9),
        "ln1_shift": gaussian(arg_keys[3], (D,), 0.5, 3.0, (), jnp.float32),
        "w_query": gaussian(arg_keys[4], (D, D), D ** -0.5, 0.21875, ((1, 4),)),
        "bias_query": gaussian(arg_keys[5], (D,), 0.5, 3.0, ((0, 4),), jnp.float32),
        "w_key": gaussian(arg_keys[6], (D, D), D ** -0.5, 0.21875, ((1, 4),)),
        "w_value": gaussian(arg_keys[7], (D, D), D ** -0.5, 0.21875, ((1, 4),)),
        "bias_value": gaussian(arg_keys[8], (D,), 0.5, 3.0, ((0, 4),), jnp.float32),
        "w_out": gaussian(arg_keys[9], (D, D), (max(1, D // 64)) ** -0.5, 1.75, ((0, 4),)),
        "bias_out": gaussian(arg_keys[10], (D,), 0.5, 3.0, (), jnp.float32),
        "ln2_gain": jnp.clip(1.0 + 0.18 * jax.random.normal(arg_keys[11], (D,), jnp.float32), 0.1, 1.9),
        "ln2_shift": gaussian(arg_keys[12], (D,), 0.5, 3.0, (), jnp.float32),
        "w_up": gaussian(arg_keys[13], (D, FF), D ** -0.5, 0.21875, ((1, 4),)),
        "bias_up": gaussian(arg_keys[14], (FF,), 0.5, 3.0, ((0, 4),), jnp.float32),
        "w_down": gaussian(arg_keys[15], (FF, D), FF ** -0.5, 0.109375, ((0, 4),)),
        "bias_down": gaussian(arg_keys[16], (D,), 0.5, 3.0, (), jnp.float32),
        "cotangent": gaussian(arg_keys[17], (TOKENS, D), 1.0, 6.0, ((0, 8),)),
    }


EPS = 1e-05
NEGATIVE = -1e+30

@jax.custom_vjp
def low(v):
    return lax.optimization_barrier(v.astype(jnp.bfloat16)).astype(jnp.float32)

@jax.custom_vjp
def low_back(v):
    return v

def low_keep(v):
    return (low(v), None)

def low_pass(kept, grad):
    return (grad,)

def back_keep(v):
    return (v, None)

def back_low(kept, grad):
    return (low(grad),)
low.defvjp(low_keep, low_pass)
low_back.defvjp(back_keep, back_low)

def precise(left_side, right_side):
    return jnp.dot(left_side, right_side, precision=lax.Precision.HIGHEST, preferred_element_type=jnp.float32)

def layer_norm(values, scale_vec, shift_vec):
    centre = values - lax.optimization_barrier(jnp.mean(values, axis=-1, keepdims=True))
    spread = lax.optimization_barrier(jnp.mean(centre * centre, axis=-1, keepdims=True))
    return centre * lax.rsqrt(spread + EPS) * scale_vec + shift_vec

def smooth_unit(values):
    return jax.nn.gelu(values, approximate=True)

def attend(pieces):
    query, keys, values, labels = pieces
    seq_length = query.shape[0]
    query_heads = query.reshape(seq_length, H, HD).transpose(1, 0, 2)
    key_heads = keys.reshape(seq_length, H, HD).transpose(1, 0, 2)
    value_heads = values.reshape(seq_length, H, HD).transpose(1, 0, 2)
    scores = jnp.einsum('hqd,hkd->hqk', query_heads, key_heads, precision=lax.Precision.HIGHEST) * HD ** (-0.5)
    scores = low_back(scores)
    positions = jnp.arange(seq_length)
    allowed = (positions[:, None] >= positions[None, :]) & (labels[:, None] == labels[None, :])
    scores = jnp.where(allowed[None], scores, NEGATIVE)
    row_top = lax.optimization_barrier(jnp.max(scores, axis=-1, keepdims=True))
    exponent = jnp.exp(scores - row_top)
    chances = low(exponent / lax.optimization_barrier(jnp.sum(exponent, axis=-1, keepdims=True)))
    mixed_heads = jnp.einsum('hqk,hkd->hqd', chances, value_heads, precision=lax.Precision.HIGHEST)
    return mixed_heads.transpose(1, 0, 2).reshape(seq_length, H * HD)

def reference(tokens_in, segments, ln1_gain, ln1_shift, w_query, bias_query, w_key, w_value, bias_value, w_out, bias_out, ln2_gain, ln2_shift, w_up, bias_up, w_down, bias_down, cotangent):

    def forward(inputs, gain_one, shift_one, wq_full, bq_full, wk_full, wv_full, bv_full, wo_full, bo_full, gain_two, shift_two, wu_full, bu_full, wd_full, bd_full):
        normed_one = low(layer_norm(inputs, gain_one, shift_one))
        query = low_back(low(precise(normed_one, wq_full) + bq_full))
        keys = low_back(low(precise(normed_one, wk_full)))
        values = low_back(low(precise(normed_one, wv_full) + bv_full))
        shaped = (query.reshape(SEQS, SEQ, D), keys.reshape(SEQS, SEQ, D), values.reshape(SEQS, SEQ, D), segments)
        attended = lax.map(jax.checkpoint(attend), shaped).reshape(TOKENS, D)
        attended = low_back(low(attended))
        hidden_one = inputs + low_back(precise(attended, wo_full)) + bo_full
        normed_two = low(layer_norm(hidden_one, gain_two, shift_two))
        pre_act = low_back(precise(normed_two, wu_full) + bu_full)
        activated = low(smooth_unit(pre_act))
        return hidden_one + low_back(precise(activated, wd_full)) + bd_full
    output, pullback = jax.vjp(forward, tokens_in.astype(jnp.float32), ln1_gain, ln1_shift, w_query.astype(jnp.float32), bias_query, w_key.astype(jnp.float32), w_value.astype(jnp.float32), bias_value, w_out.astype(jnp.float32), bias_out, ln2_gain, ln2_shift, w_up.astype(jnp.float32), bias_up, w_down.astype(jnp.float32), bias_down)
    grads = pullback(cotangent.astype(jnp.float32))
    return (output.astype(jnp.bfloat16), grads[0], grads[1], grads[2], grads[3], grads[4], grads[5], grads[6], grads[7], grads[8], grads[9], grads[10], grads[11], grads[12], grads[13], grads[14], grads[15])
```

```python
import jax
import jax.numpy as jnp
from jax import lax
from jax.sharding import PartitionSpec as P

HD = 64


EPS = 1e-05
NEGATIVE = -1e30


def layer_norm(values, scale_vec, shift_vec):
    centre = values - jnp.mean(values, axis=-1, keepdims=True)
    spread = jnp.mean(centre * centre, axis=-1, keepdims=True)
    return centre * lax.rsqrt(spread + EPS) * scale_vec + shift_vec


def smooth_unit(values):
    return jax.nn.gelu(values, approximate=True)


def matmul(left_side, right_side):
    return jnp.dot(left_side, right_side, preferred_element_type=jnp.float32)


def inner_rows(left_side, right_side):
    return lax.dot_general(
        left_side, right_side, (((0,), (0,)), ((), ())), preferred_element_type=jnp.float32
    )


def inner_cols(left_side, right_side):
    return lax.dot_general(
        left_side, right_side, (((1,), (1,)), ((), ())), preferred_element_type=jnp.float32
    )


def heads_first(values, local_heads):
    return values.reshape(values.shape[0], local_heads, HD).transpose(1, 0, 2)


def heads_last(values):
    return values.transpose(1, 0, 2).reshape(values.shape[1], values.shape[0] * values.shape[2])


def block_scores(query_block, key_heads, labels, start_row, block_rows):
    seq_length = labels.shape[0]
    row_label = labels[start_row : start_row + block_rows]
    rows_at = start_row + jnp.arange(block_rows)[:, None]
    cols_at = jnp.arange(seq_length)[None, :]
    allowed = (rows_at >= cols_at) & (row_label[:, None] == labels[None, :])
    scores = jnp.einsum(
        "hqd,hkd->hqk", query_block, key_heads, preferred_element_type=jnp.float32
    ) * HD ** (-0.5)
    return jnp.where(allowed[None], scores, NEGATIVE)


def swap(values, axis, bit):
    return lax.ppermute(values, axis, [(i, i ^ bit) for i in range(lax.axis_size(axis))])


def bits_of(axis):
    return [1 << i for i in range(lax.axis_size(axis).bit_length() - 1)]


def sum_scatter(values, axis, bits):
    me = lax.axis_index(axis)
    for bit in bits:
        half = values.shape[0] // 2
        mine = jnp.where(me & bit, 1, 0)
        sent = lax.dynamic_slice_in_dim(values, (1 - mine) * half, half, 0)
        values = lax.dynamic_slice_in_dim(values, mine * half, half, 0) + swap(sent, axis, bit)
    return values


def join(values, axis, bits):
    me = lax.axis_index(axis)
    for bit in reversed(bits):
        other = swap(values, axis, bit)
        upper = (me & bit) != 0
        values = jnp.concatenate(
            [jnp.where(upper, other, values), jnp.where(upper, values, other)], axis=0
        )
    return values


def sum_all(values, axis, bits):
    return join(sum_scatter(values, axis, bits), axis, bits)


def sum_dp(values):
    near, far = bits_of("dp")[:1], bits_of("dp")[1:]
    cut = values.shape[1] // 2
    first = sum_all(values[:, :cut], "dp", near + far)
    second = sum_all(values[:, cut:], "dp", near + far[::-1])
    return jnp.concatenate([first, second], axis=1)


def sum_tensor(values, parts):
    rows = values.shape[0] // parts
    pieces = [values[i * rows : (i + 1) * rows] for i in range(parts)]
    return jnp.concatenate([sum_all(p, "tensor", bits_of("tensor")) for p in pieces], axis=0)


def spread(values, bits):
    for bit in bits:
        values = jnp.concatenate([values, swap(values, "dp", bit)], axis=0)
    return values


def rows_of(*vectors):
    pad = jnp.zeros((64 - len(vectors), vectors[0].shape[0]), jnp.float32)
    return jnp.concatenate([jnp.stack(vectors), pad], axis=0)


def other_units(w_up, w_down, bias_up):
    size, place = lax.axis_size("dp"), lax.axis_index("dp")
    count = w_down.shape[0] // size
    up_piece = lax.dynamic_slice_in_dim(w_up, place * count, count, 1).T.astype(jnp.float32) * 2.0
    down_piece = lax.dynamic_slice_in_dim(w_down, place * count, count, 0).astype(jnp.float32) * 2.0
    near, far = bits_of("dp")[:1], bits_of("dp")[1:]
    first, second = far + near, far[::-1] + near
    biases = lax.all_gather(bias_up, "tensor").reshape(-1, size, count)
    me = lax.axis_index("tensor")
    found = []
    for offset in range(1, lax.axis_size("tensor")):
        up_own, down_own = swap(up_piece, "tensor", offset), swap(down_piece, "tensor", offset)
        bias = lax.dynamic_index_in_dim(biases, me ^ offset, 0, False)
        order = jnp.arange(1) ^ place
        for bit in first:
            order = jnp.concatenate([order, order ^ bit])
        ups, downs = spread(up_own, first), spread(down_own, first)
        first, second = second, first
        found.append((ups, downs, bias[order].reshape(-1)))
    return found


def per_device(
    tokens_in,
    segments,
    ln1_gain,
    ln1_shift,
    w_query,
    bias_query,
    w_key,
    w_value,
    bias_value,
    w_out,
    bias_out,
    ln2_gain,
    ln2_shift,
    w_up,
    bias_up,
    w_down,
    bias_down,
    cotangent,
):
    inputs = tokens_in.astype(jnp.float32)
    others = other_units(w_up, w_down, bias_up)
    local_heads = w_query.shape[1] // HD
    seq_count, seq_len = segments.shape
    block_rows = min(512, seq_len)
    normed_one, norm_one_back = jax.vjp(layer_norm, inputs, ln1_gain, ln1_shift)
    normed_low = normed_one.astype(jnp.bfloat16)
    query = (matmul(normed_low, w_query) + bias_query).astype(jnp.bfloat16)
    keys = matmul(normed_low, w_key).astype(jnp.bfloat16)
    values = (matmul(normed_low, w_value) + bias_value).astype(jnp.bfloat16)
    logsum_blocks = []
    seq_at = 0
    query_heads = heads_first(query, local_heads)
    key_heads = heads_first(keys, local_heads)
    value_heads = heads_first(values, local_heads)
    mixed_blocks = []
    for start_row in range(0, seq_len, block_rows):
        scores = block_scores(
            query_heads[:, start_row : start_row + block_rows],
            key_heads,
            segments[seq_at],
            start_row,
            block_rows,
        )
        row_top = jnp.max(scores, axis=-1, keepdims=True)
        exponent = jnp.exp(scores - row_top)
        row_total = jnp.sum(exponent, axis=-1, keepdims=True)
        chances = (exponent / row_total).astype(jnp.bfloat16)
        mixed_blocks.append(
            jnp.einsum("hqk,hkd->hqd", chances, value_heads, preferred_element_type=jnp.float32)
        )
        logsum_blocks.append(row_top + jnp.log(row_total))
    attended_seqs = heads_last(jnp.concatenate(mixed_blocks, axis=1))
    attended_low = attended_seqs.astype(jnp.bfloat16)
    attention_total = sum_tensor(matmul(attended_low, w_out), 4)
    hidden_one = inputs + attention_total + bias_out
    normed_two, norm_two_back = jax.vjp(layer_norm, hidden_one, ln2_gain, ln2_shift)
    normed_two_low = normed_two.astype(jnp.bfloat16)
    grad_out = cotangent.astype(jnp.float32)
    pre_act = matmul(normed_two_low, w_up) + bias_up
    activated, act_back = jax.vjp(smooth_unit, pre_act)
    activated_low = activated.astype(jnp.bfloat16)
    feed_total = matmul(activated_low, w_down)
    grad_w_down = inner_rows(activated_low, cotangent)
    grad_bias_down = jnp.sum(grad_out, axis=0)
    (grad_pre,) = act_back(inner_cols(cotangent, w_down))
    grad_pre_low = grad_pre.astype(jnp.bfloat16)
    grad_w_up = inner_rows(normed_two_low, grad_pre_low)
    grad_bias_up = jnp.sum(grad_pre_low.astype(jnp.float32), axis=0)
    grad_normed_two = inner_cols(grad_pre_low, w_up)
    for up_part, down_part, bias_part in others:
        up_part, down_part = (up_part * 0.5).astype(jnp.bfloat16), (down_part * 0.5).astype(jnp.bfloat16)
        pre_act = inner_cols(normed_two_low, up_part) + bias_part
        activated, act_back = jax.vjp(smooth_unit, pre_act)
        feed_total = feed_total + matmul(activated.astype(jnp.bfloat16), down_part)
        (grad_pre,) = act_back(inner_cols(cotangent, down_part))
        grad_normed_two = grad_normed_two + matmul(grad_pre.astype(jnp.bfloat16), up_part)
    output = (hidden_one + feed_total + bias_down).astype(jnp.bfloat16)
    grad_hidden_part, grad_ln2_gain, grad_ln2_shift = norm_two_back(grad_normed_two)
    grad_hidden = grad_out + grad_hidden_part
    units = w_up.shape[1]
    total = sum_dp(
        jnp.concatenate(
            [
                grad_w_up,
                grad_w_down,
                rows_of(grad_ln2_gain, grad_ln2_shift, grad_bias_up, grad_bias_down),
            ],
            axis=0,
        )
    )
    width = w_up.shape[0]
    grad_w_up, grad_w_down = total[:width], total[width : width + units]
    grad_ln2_gain, grad_ln2_shift, grad_bias_up, grad_bias_down = total[
        width + units : width + units + 4
    ]
    grad_hidden_low = grad_hidden.astype(jnp.bfloat16)
    grad_w_out = inner_rows(attended_low, grad_hidden_low)
    grad_bias_out = jnp.sum(grad_hidden, axis=0)
    grad_attended_low = inner_cols(grad_hidden_low, w_out).astype(jnp.bfloat16)
    block_count = 0
    seq_at = 0
    query_heads = heads_first(query, local_heads)
    key_heads = heads_first(keys, local_heads)
    value_heads = heads_first(values, local_heads)
    grad_heads = heads_first(grad_attended_low, local_heads)
    grad_key_heads = jnp.zeros(key_heads.shape, jnp.float32)
    grad_value_heads = jnp.zeros(value_heads.shape, jnp.float32)
    grad_query_blocks = []
    for start_row in range(0, seq_len, block_rows):
        query_block = query_heads[:, start_row : start_row + block_rows]
        grad_block = grad_heads[:, start_row : start_row + block_rows]
        scores = block_scores(query_block, key_heads, segments[seq_at], start_row, block_rows)
        chances_full = jnp.exp(scores - logsum_blocks[block_count])
        block_count = block_count + 1
        grad_chances = jnp.einsum(
            "hqd,hkd->hqk", grad_block, value_heads, preferred_element_type=jnp.float32
        )
        centre = jnp.sum(chances_full * grad_chances, axis=-1, keepdims=True)
        grad_scores = (chances_full * (grad_chances - centre)).astype(jnp.bfloat16)
        grad_query_blocks.append(
            jnp.einsum("hqk,hkd->hqd", grad_scores, key_heads, preferred_element_type=jnp.float32)
            * HD ** (-0.5)
        )
        grad_key_heads = grad_key_heads + jnp.einsum(
            "hqk,hqd->hkd", grad_scores, query_block, preferred_element_type=jnp.float32
        ) * HD ** (-0.5)
        grad_value_heads = grad_value_heads + jnp.einsum(
            "hqk,hqd->hkd",
            chances_full.astype(jnp.bfloat16),
            grad_block,
            preferred_element_type=jnp.float32,
        )
    grad_query_seqs = heads_last(jnp.concatenate(grad_query_blocks, axis=1))
    grad_key_seqs = heads_last(grad_key_heads)
    grad_value_seqs = heads_last(grad_value_heads)
    grad_query_low = grad_query_seqs.astype(jnp.bfloat16)
    grad_key_low = grad_key_seqs.astype(jnp.bfloat16)
    grad_value_low = grad_value_seqs.astype(jnp.bfloat16)
    grad_normed_part = (
        inner_cols(grad_query_low, w_query)
        + inner_cols(grad_key_low, w_key)
        + inner_cols(grad_value_low, w_value)
    )
    grad_normed_one = sum_tensor(grad_normed_part, 4)
    grad_bias_query = jnp.sum(grad_query_low.astype(jnp.float32), axis=0)
    grad_bias_value = jnp.sum(grad_value_low.astype(jnp.float32), axis=0)
    _, grad_ln1_gain, grad_ln1_shift = norm_one_back(grad_normed_part)
    held = w_query.shape[1]
    width = w_query.shape[0]
    head_bias = jnp.zeros((width,), jnp.float32)
    head_bias = head_bias.at[:held].set(grad_bias_query).at[held : 2 * held].set(grad_bias_value)
    total = sum_dp(
        jnp.concatenate(
            [
                inner_rows(grad_query_low, normed_low),
                inner_rows(grad_key_low, normed_low),
                inner_rows(grad_value_low, normed_low),
                grad_w_out,
                rows_of(grad_ln1_gain, grad_ln1_shift, grad_bias_out, head_bias),
            ],
            axis=0,
        )
    )
    grad_w_query = total[:held].T
    grad_w_key = total[held : 2 * held].T
    grad_w_value = total[2 * held : 3 * held].T
    grad_w_out = total[3 * held : 4 * held]
    grad_ln1_gain, grad_ln1_shift = lax.psum(total[4 * held : 4 * held + 2], "tensor")
    grad_bias_out = total[4 * held + 2]
    grad_bias_query = total[4 * held + 3, :held]
    grad_bias_value = total[4 * held + 3, held : 2 * held]
    grad_input_part, _, _ = norm_one_back(grad_normed_one)
    grad_input = grad_hidden + grad_input_part
    return (
        output,
        grad_input,
        grad_ln1_gain,
        grad_ln1_shift,
        grad_w_query,
        grad_bias_query,
        grad_w_key,
        grad_w_value,
        grad_bias_value,
        grad_w_out,
        grad_bias_out,
        grad_ln2_gain,
        grad_ln2_shift,
        grad_w_up,
        grad_bias_up,
        grad_w_down,
        grad_bias_down,
    )


def solution(mesh):
    in_specs = (
        P("dp", None),
        P("dp", None),
        P(),
        P(),
        P(None, "tensor"),
        P("tensor"),
        P(None, "tensor"),
        P(None, "tensor"),
        P("tensor"),
        P("tensor", None),
        P(),
        P(),
        P(),
        P(None, "tensor"),
        P("tensor"),
        P("tensor", None),
        P(),
        P("dp", None),
    )
    out_specs = (
        P("dp", None),
        P("dp", None),
        P(),
        P(),
        P(None, "tensor"),
        P("tensor"),
        P(None, "tensor"),
        P(None, "tensor"),
        P("tensor"),
        P("tensor", None),
        P(),
        P(),
        P(),
        P(None, "tensor"),
        P("tensor"),
        P("tensor", None),
        P(),
    )
    return jax.shard_map(
        per_device, mesh=mesh, in_specs=in_specs, out_specs=out_specs, check_vma=False
    )
```

```python
import jax
import jax.numpy as jnp
from jax import lax
from jax.experimental import pallas as pl
from jax.experimental.pallas import tpu as pltpu
from jax.sharding import PartitionSpec as P

HD = 64


EPS = 1e-05
NEGATIVE = -1e30


def layer_norm(values, scale_vec, shift_vec):
    centre = values - jnp.mean(values, axis=-1, keepdims=True)
    spread = jnp.mean(centre * centre, axis=-1, keepdims=True)
    return centre * lax.rsqrt(spread + EPS) * scale_vec + shift_vec


def smooth_unit(values):
    return jax.nn.gelu(values, approximate=True)


def matmul(left_side, right_side):
    return jnp.dot(left_side, right_side, preferred_element_type=jnp.float32)


def inner_rows(left_side, right_side):
    return lax.dot_general(
        left_side, right_side, (((0,), (0,)), ((), ())), preferred_element_type=jnp.float32
    )


def inner_cols(left_side, right_side):
    return lax.dot_general(
        left_side, right_side, (((1,), (1,)), ((), ())), preferred_element_type=jnp.float32
    )


def heads_first(values, local_heads):
    return values.reshape(values.shape[0], local_heads, HD).transpose(1, 0, 2)


def heads_last(values):
    return values.transpose(1, 0, 2).reshape(values.shape[1], values.shape[0] * values.shape[2])


def block_scores(query_block, key_heads, labels, start_row, block_rows):
    seq_length = labels.shape[0]
    row_label = labels[start_row : start_row + block_rows]
    rows_at = start_row + jnp.arange(block_rows)[:, None]
    cols_at = jnp.arange(seq_length)[None, :]
    allowed = (rows_at >= cols_at) & (row_label[:, None] == labels[None, :])
    scores = jnp.einsum(
        "hqd,hkd->hqk", query_block, key_heads, preferred_element_type=jnp.float32
    ) * HD ** (-0.5)
    return jnp.where(allowed[None], scores, NEGATIVE)


def bits_of(size):
    return [1 << i for i in range(size.bit_length() - 1)]


def bit_of(axis, bit):
    return (lax.axis_index(axis) // bit) % 2


def partner(axis, bit):
    me = lax.axis_index(axis)
    for one in bits_of(lax.axis_size(axis)):
        if bit & one:
            me = me + one - 2 * one * bit_of(axis, one)
    return {axis: me}


def greet(partners):
    barrier = pltpu.get_barrier_semaphore()
    for device in partners:
        pl.semaphore_signal(
            barrier, inc=1, device_id=device, device_id_type=pl.DeviceIdType.MESH
        )
    pl.semaphore_wait(barrier, len(partners))


class Copies:
    def __init__(self, send_sems, recv_sems):
        self.sems, self.used = (send_sems, recv_sems), 0

    def start(self, source, target, device):
        at, self.used = self.used, self.used + 1
        copy = pltpu.make_async_remote_copy(
            src_ref=source,
            dst_ref=target,
            send_sem=self.sems[0].at[at],
            recv_sem=self.sems[1].at[at],
            device_id=device,
            device_id_type=pl.DeviceIdType.MESH,
        )
        copy.start()
        return copy


def sum_stream(copies, source, acc, recv, first, rows, steps):
    base, at, held = first, 0, []
    origin, start = source, first
    for number, (axis, bit) in enumerate(steps):
        half = rows >> (number + 1)
        mine = bit_of(axis, bit)
        keep = pl.multiple_of(start + mine * half, 8)
        give = pl.multiple_of(start + (1 - mine) * half, 8)
        landing = recv.at[pl.ds(at, half)]
        copy = copies.start(origin.at[pl.ds(give, half)], landing, partner(axis, bit))
        yield
        copy.wait()
        recv[pl.ds(at, half), :] = recv[pl.ds(at, half), :] + origin[pl.ds(keep, half), :]
        base = pl.multiple_of(base + mine * half, 8)
        origin, start, at = recv, at, at + half
        held.append((base, half))
    acc[pl.ds(base, half), :] = recv[pl.ds(start, half), :]
    for (axis, bit), (keep, half) in zip(reversed(steps), reversed(held)):
        window = acc.at[pl.ds(keep, half)]
        copy = copies.start(window, window, partner(axis, bit))
        yield
        copy.wait()


def run_streams(streams):
    streams = list(streams)
    while streams:
        streams = [stream for stream in streams if next(stream, streams) is not streams]


PARTS = 4
MESH_PARAMS = dict(has_side_effects=True, vmem_limit_bytes=56 * 2**20)


def tensor_streams(copies, source, acc, recv, bits):
    rows = acc.shape[0] // PARTS
    return [
        sum_stream(
            copies,
            source,
            acc,
            recv.at[pl.ds(part * rows, rows)],
            part * rows,
            rows,
            [("tensor", bit) for bit in bits],
        )
        for part in range(PARTS)
    ]


def front_kernel(
    dp_bits, t_bits, part_ref, up_ref, down_ref, bias_ref, sum_ref, ups_ref, downs_ref,
    biases_ref, recv, wide, send_sems, recv_sems,
):
    greet(
        [partner("tensor", b) for b in range(1, biases_ref.shape[0] + 1)]
        + [partner("dp", b) for b in dp_bits]
    )
    copies = Copies(send_sems, recv_sems)
    others = biases_ref.shape[0]
    near, far = dp_bits[:1], dp_bits[1:]
    count = up_ref.shape[0]

    def gather(kind, other, piece, done):
        lead = 1 << (other.bit_length() - 1)
        rest = other - lead
        place = wide.at[kind, other - 1]
        if rest == 0:
            origin, link = piece, lead
        else:
            while lead not in done:
                yield
            origin, link = wide.at[kind, lead - 1, pl.ds(0, count)], rest
        copy = copies.start(origin, place.at[pl.ds(0, count)], partner("tensor", link))
        yield
        copy.wait()
        done.add(other)
        rows = count
        order = (far if other % 2 else far[::-1]) + near
        for bit in order:
            copy = copies.start(
                place.at[pl.ds(0, rows)], place.at[pl.ds(rows, rows)], partner("dp", bit)
            )
            yield
            copy.wait()
            rows = 2 * rows
        out = (ups_ref, downs_ref)[kind]

        def narrow(step, carry):
            window = pl.ds(pl.multiple_of(step * 32, 32), 32)
            out[other - 1, window, :] = wide[kind, other - 1, window, :].astype(jnp.bfloat16)
            return carry

        lax.fori_loop(0, rows // 32, narrow, 0)

    def bias_stream(other):
        copy = copies.start(bias_ref, biases_ref.at[other - 1], partner("tensor", other))
        yield
        copy.wait()

    done = (set(), set())
    run_streams(
        [gather(0, o, up_ref, done[0]) for o in range(1, others + 1)]
        + [gather(1, o, down_ref, done[1]) for o in range(1, others + 1)]
        + tensor_streams(copies, part_ref, sum_ref, recv, t_bits)
        + [bias_stream(o) for o in range(1, others + 1)]
    )


def unit_order(other, size):
    bits = bits_of(size)
    near, far = bits[:1], bits[1:]
    order = jnp.arange(1) ^ (lax.axis_index("dp") % size)
    for bit in (far if other % 2 else far[::-1]) + near:
        order = jnp.concatenate([order, order ^ bit])
    return order


def front(partial, w_up, w_down, bias_up):
    others = lax.axis_size("tensor") - 1
    units, width = w_down.shape
    size = lax.axis_size("dp")
    while units % (8 * size):
        size = size // 2
    place, count = lax.axis_index("dp") % size, units // size
    up_piece = lax.dynamic_slice_in_dim(w_up, place * count, count, 1).T.astype(jnp.float32)
    down_piece = lax.dynamic_slice_in_dim(w_down, place * count, count, 0).astype(jnp.float32)
    bias_block = jnp.broadcast_to(bias_up[None], (8, units))
    dp_bits, t_bits = bits_of(size), bits_of(others + 1)
    total_copies = 2 * others * (1 + len(dp_bits)) + others + PARTS * 2 * len(t_bits)
    vmem = pl.BlockSpec(memory_space=pltpu.VMEM)

    def body(*refs):
        front_kernel(dp_bits, t_bits, *refs)

    total, ups, downs, biases = pl.pallas_call(
        body,
        out_shape=[
            jax.ShapeDtypeStruct(partial.shape, jnp.float32),
            jax.ShapeDtypeStruct((others, units, width), jnp.bfloat16),
            jax.ShapeDtypeStruct((others, units, width), jnp.bfloat16),
            jax.ShapeDtypeStruct((others, 8, units), jnp.float32),
        ],
        in_specs=[vmem] * 4,
        out_specs=[vmem] * 4,
        scratch_shapes=[
            pltpu.VMEM(partial.shape, jnp.float32),
            pltpu.VMEM((2, others, units, width), jnp.float32),
            pltpu.SemaphoreType.DMA((total_copies,)),
            pltpu.SemaphoreType.DMA((total_copies,)),
        ],
        compiler_params=pltpu.CompilerParams(collective_id=0, **MESH_PARAMS),
    )(partial, up_piece, down_piece, bias_block)
    found = []
    for other in range(1, others + 1):
        bias = biases[other - 1, 0].reshape(size, count)[unit_order(other, size)].reshape(-1)
        found.append((ups[other - 1], downs[other - 1], bias))
    return total, found


def back_kernel(
    dp_bits, t_bits, part_ref, *refs,
):
    count = (len(refs) - 9) // 2
    given, sum_ref, wanted = refs[:count], refs[count], refs[count + 1 : 2 * count + 1]
    acc, loaded, recv, dp_recv, small_recv, send_sems, recv_sems, local_sems = refs[2 * count + 1 :]
    loads, at = [], 0
    for number, ref in enumerate(given):
        rows = ref.shape[0]
        loads.append(
            pltpu.make_async_copy(ref, loaded.at[pl.ds(at, rows)], local_sems.at[number])
        )
        at = at + rows
    for load in loads:
        load.start()
    greet([partner("tensor", b) for b in t_bits] + [partner("dp", b) for b in dp_bits])
    copies = Copies(send_sems, recv_sems)
    near, far = dp_bits[:1], dp_bits[1:]
    half = acc.shape[0] // 2

    def dp_stream(part):
        order = near + (far if part == 0 else far[::-1])
        return sum_stream(
            copies,
            loaded,
            acc,
            dp_recv.at[pl.ds(part * half, half)],
            part * half,
            half,
            [("dp", bit) for bit in order],
        )

    def last_stream():
        yield from dp_stream(1)
        rows = pl.ds(acc.shape[0] - given[-1].shape[0], 8)
        for number, bit in enumerate(t_bits):
            copy = copies.start(acc.at[rows], small_recv.at[number], partner("tensor", bit))
            yield
            copy.wait()
            acc[rows, :] = acc[rows, :] + small_recv[number]

    streams = tensor_streams(copies, part_ref, sum_ref, recv, t_bits)
    for stream in streams:
        next(stream)
    for load in loads:
        load.wait()
    run_streams([dp_stream(0), last_stream()] + streams)
    stores, at = [], 0
    for number, ref in enumerate(wanted):
        rows = ref.shape[0]
        stores.append(
            pltpu.make_async_copy(acc.at[pl.ds(at, rows)], ref, local_sems.at[count + number])
        )
        at = at + rows
    for store in stores:
        store.start()
    for store in stores:
        store.wait()


def back(partial, blocks):
    unit = 16 * lax.axis_size("dp")
    short = -sum(block.shape[0] for block in blocks) % unit
    blocks = [*blocks[:-1], jnp.pad(blocks[-1], ((0, short), (0, 0)))]
    dp_bits, t_bits = bits_of(lax.axis_size("dp")), bits_of(lax.axis_size("tensor"))
    rows = sum(block.shape[0] for block in blocks)
    width = partial.shape[1]
    total_copies = PARTS * 2 * len(t_bits) + 4 * len(dp_bits) + len(t_bits)
    vmem, anywhere = pl.BlockSpec(memory_space=pltpu.VMEM), pl.BlockSpec(memory_space=pl.ANY)

    def body(*refs):
        back_kernel(dp_bits, t_bits, *refs)

    return pl.pallas_call(
        body,
        out_shape=[jax.ShapeDtypeStruct(v.shape, jnp.float32) for v in (partial, *blocks)],
        in_specs=[vmem] + [anywhere] * len(blocks),
        out_specs=[vmem] + [anywhere] * len(blocks),
        scratch_shapes=[
            pltpu.VMEM((rows, width), jnp.float32),
            pltpu.VMEM((rows, width), jnp.float32),
            pltpu.VMEM(partial.shape, jnp.float32),
            pltpu.VMEM((rows, width), jnp.float32),
            pltpu.VMEM((len(t_bits), 8, width), jnp.float32),
            pltpu.SemaphoreType.DMA((total_copies,)),
            pltpu.SemaphoreType.DMA((total_copies,)),
            pltpu.SemaphoreType.DMA((2 * len(blocks),)),
        ],
        compiler_params=pltpu.CompilerParams(collective_id=1, **MESH_PARAMS),
    )(partial, *blocks)


def per_device(
    tokens_in,
    segments,
    ln1_gain,
    ln1_shift,
    w_query,
    bias_query,
    w_key,
    w_value,
    bias_value,
    w_out,
    bias_out,
    ln2_gain,
    ln2_shift,
    w_up,
    bias_up,
    w_down,
    bias_down,
    cotangent,
):
    inputs = tokens_in.astype(jnp.float32)
    local_heads = w_query.shape[1] // HD
    seq_count, seq_len = segments.shape
    block_rows = min(512, seq_len)
    normed_one, norm_one_back = jax.vjp(layer_norm, inputs, ln1_gain, ln1_shift)
    normed_low = normed_one.astype(jnp.bfloat16)
    query = (matmul(normed_low, w_query) + bias_query).astype(jnp.bfloat16)
    keys = matmul(normed_low, w_key).astype(jnp.bfloat16)
    values = (matmul(normed_low, w_value) + bias_value).astype(jnp.bfloat16)
    logsum_blocks = []
    seq_at = 0
    query_heads = heads_first(query, local_heads)
    key_heads = heads_first(keys, local_heads)
    value_heads = heads_first(values, local_heads)
    mixed_blocks = []
    for start_row in range(0, seq_len, block_rows):
        scores = block_scores(
            query_heads[:, start_row : start_row + block_rows],
            key_heads,
            segments[seq_at],
            start_row,
            block_rows,
        )
        row_top = jnp.max(scores, axis=-1, keepdims=True)
        exponent = jnp.exp(scores - row_top)
        row_total = jnp.sum(exponent, axis=-1, keepdims=True)
        chances = (exponent / row_total).astype(jnp.bfloat16)
        mixed_blocks.append(
            jnp.einsum("hqk,hkd->hqd", chances, value_heads, preferred_element_type=jnp.float32)
        )
        logsum_blocks.append(row_top + jnp.log(row_total))
    attended_seqs = heads_last(jnp.concatenate(mixed_blocks, axis=1))
    attended_low = attended_seqs.astype(jnp.bfloat16)
    attention_total, others = front(matmul(attended_low, w_out), w_up, w_down, bias_up)
    hidden_one = inputs + attention_total + bias_out
    normed_two, norm_two_back = jax.vjp(layer_norm, hidden_one, ln2_gain, ln2_shift)
    normed_two_low = normed_two.astype(jnp.bfloat16)
    grad_out = cotangent.astype(jnp.float32)
    pre_act = matmul(normed_two_low, w_up) + bias_up
    activated, act_back = jax.vjp(smooth_unit, pre_act)
    activated_low = activated.astype(jnp.bfloat16)
    feed_total = matmul(activated_low, w_down)
    grad_w_down = inner_rows(activated_low, cotangent)
    grad_bias_down = jnp.sum(grad_out, axis=0)
    (grad_pre,) = act_back(inner_cols(cotangent, w_down))
    grad_pre_low = grad_pre.astype(jnp.bfloat16)
    grad_w_up = inner_rows(normed_two_low, grad_pre_low)
    grad_bias_up = jnp.sum(grad_pre_low.astype(jnp.float32), axis=0)
    grad_normed_two = inner_cols(grad_pre_low, w_up)
    for up_part, down_part, bias_part in others:
        pre_act = inner_cols(normed_two_low, up_part) + bias_part
        activated, act_back = jax.vjp(smooth_unit, pre_act)
        feed_total = feed_total + matmul(activated.astype(jnp.bfloat16), down_part)
        (grad_pre,) = act_back(inner_cols(cotangent, down_part))
        grad_normed_two = grad_normed_two + matmul(grad_pre.astype(jnp.bfloat16), up_part)
    output = (hidden_one + feed_total + bias_down).astype(jnp.bfloat16)
    grad_hidden_part, grad_ln2_gain, grad_ln2_shift = norm_two_back(grad_normed_two)
    grad_hidden = grad_out + grad_hidden_part
    grad_hidden_low = grad_hidden.astype(jnp.bfloat16)
    grad_w_out = inner_rows(attended_low, grad_hidden_low)
    grad_bias_out = jnp.sum(grad_hidden, axis=0)
    grad_attended_low = inner_cols(grad_hidden_low, w_out).astype(jnp.bfloat16)
    block_count = 0
    seq_at = 0
    query_heads = heads_first(query, local_heads)
    key_heads = heads_first(keys, local_heads)
    value_heads = heads_first(values, local_heads)
    grad_heads = heads_first(grad_attended_low, local_heads)
    grad_key_heads = jnp.zeros(key_heads.shape, jnp.float32)
    grad_value_heads = jnp.zeros(value_heads.shape, jnp.float32)
    grad_query_blocks = []
    for start_row in range(0, seq_len, block_rows):
        query_block = query_heads[:, start_row : start_row + block_rows]
        grad_block = grad_heads[:, start_row : start_row + block_rows]
        scores = block_scores(query_block, key_heads, segments[seq_at], start_row, block_rows)
        chances_full = jnp.exp(scores - logsum_blocks[block_count])
        block_count = block_count + 1
        grad_chances = jnp.einsum(
            "hqd,hkd->hqk", grad_block, value_heads, preferred_element_type=jnp.float32
        )
        centre = jnp.sum(chances_full * grad_chances, axis=-1, keepdims=True)
        grad_scores = (chances_full * (grad_chances - centre)).astype(jnp.bfloat16)
        grad_query_blocks.append(
            jnp.einsum("hqk,hkd->hqd", grad_scores, key_heads, preferred_element_type=jnp.float32)
            * HD ** (-0.5)
        )
        grad_key_heads = grad_key_heads + jnp.einsum(
            "hqk,hqd->hkd", grad_scores, query_block, preferred_element_type=jnp.float32
        ) * HD ** (-0.5)
        grad_value_heads = grad_value_heads + jnp.einsum(
            "hqk,hqd->hkd",
            chances_full.astype(jnp.bfloat16),
            grad_block,
            preferred_element_type=jnp.float32,
        )
    grad_query_seqs = heads_last(jnp.concatenate(grad_query_blocks, axis=1))
    grad_key_seqs = heads_last(grad_key_heads)
    grad_value_seqs = heads_last(grad_value_heads)
    grad_query_low = grad_query_seqs.astype(jnp.bfloat16)
    grad_key_low = grad_key_seqs.astype(jnp.bfloat16)
    grad_value_low = grad_value_seqs.astype(jnp.bfloat16)
    grad_normed_part = (
        inner_cols(grad_query_low, w_query)
        + inner_cols(grad_key_low, w_key)
        + inner_cols(grad_value_low, w_value)
    )
    grad_bias_query = jnp.sum(grad_query_low.astype(jnp.float32), axis=0)
    grad_bias_value = jnp.sum(grad_value_low.astype(jnp.float32), axis=0)
    _, grad_ln1_gain, grad_ln1_shift = norm_one_back(grad_normed_part)
    held, width = w_query.shape[1], w_query.shape[0]
    head_bias = jnp.concatenate(
        [grad_bias_query, grad_bias_value, jnp.zeros((width - 2 * held,), jnp.float32)]
    )
    small = jnp.concatenate(
        [
            jnp.stack([grad_ln1_gain, grad_ln1_shift]),
            jnp.zeros((6, width), jnp.float32),
            jnp.stack(
                [
                    grad_bias_out,
                    head_bias,
                    grad_ln2_gain,
                    grad_ln2_shift,
                    grad_bias_up,
                    grad_bias_down,
                ]
            ),
            jnp.zeros((2, width), jnp.float32),
        ]
    )
    (
        grad_normed_one,
        grad_w_up,
        grad_w_down,
        grad_w_query,
        grad_w_key,
        grad_w_value,
        grad_w_out,
        small,
    ) = back(
        grad_normed_part,
        [
            grad_w_up,
            grad_w_down,
            inner_rows(grad_query_low, normed_low),
            inner_rows(grad_key_low, normed_low),
            inner_rows(grad_value_low, normed_low),
            grad_w_out,
            small,
        ],
    )
    grad_w_query, grad_w_key, grad_w_value = grad_w_query.T, grad_w_key.T, grad_w_value.T
    grad_ln1_gain, grad_ln1_shift = small[0], small[1]
    grad_bias_out = small[8]
    grad_bias_query, grad_bias_value = small[9, :held], small[9, held : 2 * held]
    grad_ln2_gain, grad_ln2_shift, grad_bias_up, grad_bias_down = small[10:14]
    grad_input_part, _, _ = norm_one_back(grad_normed_one)
    grad_input = grad_hidden + grad_input_part
    return (
        output,
        grad_input,
        grad_ln1_gain,
        grad_ln1_shift,
        grad_w_query,
        grad_bias_query,
        grad_w_key,
        grad_w_value,
        grad_bias_value,
        grad_w_out,
        grad_bias_out,
        grad_ln2_gain,
        grad_ln2_shift,
        grad_w_up,
        grad_bias_up,
        grad_w_down,
        grad_bias_down,
    )


def solution(mesh):
    in_specs = (
        P("dp", None),
        P("dp", None),
        P(),
        P(),
        P(None, "tensor"),
        P("tensor"),
        P(None, "tensor"),
        P(None, "tensor"),
        P("tensor"),
        P("tensor", None),
        P(),
        P(),
        P(),
        P(None, "tensor"),
        P("tensor"),
        P("tensor", None),
        P(),
        P("dp", None),
    )
    out_specs = (
        P("dp", None),
        P("dp", None),
        P(),
        P(),
        P(None, "tensor"),
        P("tensor"),
        P(None, "tensor"),
        P(None, "tensor"),
        P("tensor"),
        P("tensor", None),
        P(),
        P(),
        P(),
        P(None, "tensor"),
        P("tensor"),
        P("tensor", None),
        P(),
    )
    return jax.shard_map(
        per_device, mesh=mesh, in_specs=in_specs, out_specs=out_specs, check_vma=False
    )
```
